512 devices in a mesh: replica: 64 (over x, z_hi, y, core), tp: 8 (over z_lo).
Axes of the slice: x: 4, y: 4, z: 16 (z_hi: 2, z_lo: 8; z = z_hi * 8 + z_lo), core: 2. Of those that a mesh axis runs over, the one named last changes fastest.
Arguments:
- decode_token_index: int32 [256, 4], P('replica'), may hold values from 0 to 76799
- token_embedding_table: bfloat16 [76800, 4096], P('replica', 'tp')
- input_norm_scale: bfloat16 [4096], P('tp'), may hold values from 0.099609375 to 1.8984375
- projection_weight: bfloat16 [2, 4096, 512], P(None, 'tp'), may hold values from -0.09375 to 0.09375
- input_factor: bfloat16 [2, 64, 4096], P(None, 'replica', 'tp'), may hold values from -0.09375 to 0.09375
- output_factor: bfloat16 [2, 512, 64], P(None, None, 'replica'), may hold values from -0.75 to 0.75
- cache: bfloat16 [2, 256, 2048, 512], P(None, 'replica', 'tp')
- cache_length_rows: int32 [256], P('replica'), may hold values from 2 to 2048, as said below
- queries: bfloat16 [256, 4, 4096], P('replica')
Outputs:
- attended: bfloat16 [256, 4, 4096], P('replica')
- new_kv: bfloat16 [2, 256, 4, 512], P(None, 'replica')
The draws below stay inside these ranges and needn't reach their ends.
Inputs may be any that keep to these rules, and one draw needn't show every extreme that they name: `cache_length_rows`: every row has at least 2 cached positions; some row holds all 2048.
All inputs are finite; a program needn't handle non-finite values.
Results may differ from the reference program's by a relative error of at most 0.0066.
Values may be sent and summed in bfloat16 or wider, within the bound.
A program may use at most 64 MiB of HBM per device.

```python
import math
import jax
import jax.numpy as jnp
import numpy as np
from jax import lax

MODEL_FEATURES = 4096
KVH = 4
QH = 32
HD = 128
FACTOR_RANK = 64
STEPS = 4
CACHE = 2048
VOCAB = 76800
ALLROWS = 256
KEY_FEATURES = 512


def draw_token_embedding_table(key, part):
    key = jax.random.fold_in(key, 3)
    key_z, key_col, key_row = jax.random.split(key, 3)
    column = jnp.exp(jax.random.uniform(key_col, (MODEL_FEATURES,), jnp.float32) * math.log(10.0))
    column = column * jnp.exp(jnp.arange(MODEL_FEATURES, dtype=jnp.float32) * (math.log(3.0) / MODEL_FEATURES))
    row_scale = jnp.exp(jax.random.uniform(key_row, (VOCAB, 1), jnp.float32) * math.log(10.0))
    entries = jax.random.normal(key_z, (VOCAB, MODEL_FEATURES), jnp.float32)
    return (0.3 * entries * column[None, :] * row_scale).astype(jnp.bfloat16)


def draw_cache_length_rows(key, part):
    key = jax.random.fold_in(key, 7)
    key_len, key_top = jax.random.split(key)
    lengths = jax.random.randint(key_len, (ALLROWS,), 2, CACHE + 1)
    chosen = jax.random.randint(key_top, (), 0, ALLROWS)
    return jnp.where(jnp.arange(ALLROWS) == chosen, CACHE, lengths).astype(jnp.int32)


def draw_cache(key, part):
    key = jax.random.fold_in(key, 11)
    base = jax.random.normal(key, (2, ALLROWS, CACHE, KEY_FEATURES), jnp.float32)
    return base.astype(jnp.bfloat16)


def draw_queries(key, part):
    key = jax.random.fold_in(key, 5)
    values = jax.random.normal(key, (ALLROWS, STEPS, QH * HD), jnp.float32)
    return values.astype(jnp.bfloat16)


def touch_ends(values, rng, least, high):
    index_at = [jax.random.randint(jax.random.fold_in(rng, axis), (), 0, length) for axis, length in enumerate(values.shape)]
    main_axis = values.shape.index(max(values.shape))
    next_to = index_at[:main_axis] + [(index_at[main_axis] + 1) % values.shape[main_axis]] + index_at[main_axis + 1:]
    return values.at[tuple(index_at)].set(least).at[tuple(next_to)].set(high)


def level_of(rng, shape, cuts, low, largest):
    gain = 1.0
    for axis_at, parts in cuts:
        draws = jax.random.uniform(jax.random.fold_in(jax.random.fold_in(rng, 6), axis_at), (parts,), jnp.float32, low / len(cuts), largest / len(cuts))
        gain = gain * jnp.repeat(jnp.exp(draws), shape[axis_at] // parts).reshape((-1,) + (1,) * (len(shape) - 1 - axis_at))
    return gain


def skewed_wide(rng, extent, amount, skew):
    weights = [min(1 << octave, amount + 1 - (1 << octave)) * (1 << 20) // math.isqrt((1 << octave) ** skew) + 1 for octave in range((amount + 1).bit_length()) if 1 << octave <= amount]
    scale = 1 + sum(weights) // (1 << 30)
    grid = np.cumsum(np.array([max(1, weight // scale) for weight in weights]))
    pick = jax.random.randint(jax.random.fold_in(rng, 1), extent, 0, int(grid[len(weights) - 1]))
    start = jnp.left_shift(1, jnp.searchsorted(jnp.asarray(grid, jnp.int32), pick, side="right").astype(jnp.int32))
    grade = start - 1 + jax.random.randint(jax.random.fold_in(rng, 4), extent, 0, 1 << 30) % jnp.minimum(start, amount + 1 - start)
    return jax.random.permutation(jax.random.fold_in(rng, 2), amount)[grade].astype(jnp.int32)


def bell_draw(rng, extent, scale, reach, shards=(), held_as=jnp.bfloat16):
    array = jax.random.normal(rng, extent, jnp.float32) * scale
    if len(shards) > 0:
        array = level_of(rng, extent, shards, -0.22, 0.18) * array
    return jnp.clip(array, min=-reach, max=reach).astype(held_as)


def setup_inputs(seed: int = 0) -> dict:
    streams_of = jax.random.split(jax.random.key(seed), 10)
    decode_token_index = touch_ends(skewed_wide(streams_of[0], (ALLROWS, STEPS), VOCAB, 2), jax.random.fold_in(streams_of[0], 3), 0, VOCAB - 1).astype(jnp.int32)
    token_embedding_table = draw_token_embedding_table(jax.random.fold_in(streams_of[9], 71), 0)
    input_norm_scale = jnp.clip(1.0 + 0.18 * jax.random.normal(streams_of[2], (MODEL_FEATURES,), jnp.float32), 0.099609375, 1.8984375).astype(jnp.bfloat16)
    projection_weight = bell_draw(streams_of[3], (2, MODEL_FEATURES, KEY_FEATURES), MODEL_FEATURES ** -0.5, 0.09375, ((1, 8),))
    input_factor = bell_draw(streams_of[4], (2, FACTOR_RANK, MODEL_FEATURES), MODEL_FEATURES ** -0.5, 0.09375, ((1, 64), (2, 8)))
    output_factor = bell_draw(streams_of[5], (2, KEY_FEATURES, FACTOR_RANK), FACTOR_RANK ** -0.5, 0.75, ((2, 64),))
    cache = draw_cache(jax.random.fold_in(streams_of[9], 71), 0)
    cache_length_rows = draw_cache_length_rows(jax.random.fold_in(streams_of[9], 71), 0)
    queries = draw_queries(jax.random.fold_in(streams_of[9], 71), 0)
    return dict(decode_token_index=decode_token_index, token_embedding_table=token_embedding_table, input_norm_scale=input_norm_scale, projection_weight=projection_weight, input_factor=input_factor, output_factor=output_factor, cache=cache, cache_length_rows=cache_length_rows, queries=queries)


ROPE_THETA = 1000000.0
NEG = -1e+30
EPS = 1e-06

def rotate(keys, positions):
    half = HD // 2
    index = jnp.arange(half, dtype=jnp.float32)
    freq = jnp.exp(index * (-2.0 * math.log(ROPE_THETA) / HD))
    angle = positions.astype(jnp.float32)[..., None] * freq
    cosine = jnp.cos(angle)[..., None, :]
    sine = jnp.sin(angle)[..., None, :]
    shaped = keys.reshape(keys.shape[:-1] + (KVH, HD))
    first = shaped[..., :half]
    second = shaped[..., half:]
    turned = jnp.concatenate([first * cosine - second * sine, second * cosine + first * sine], axis=-1)
    return turned.reshape(keys.shape)

def attend_row(items):
    query, cached_keys, cached_values, fresh_keys, fresh_values, length = items
    group = QH // KVH
    scale = 1.0 / math.sqrt(HD)
    q_all = query.astype(jnp.float32).reshape(STEPS, KVH, group, HD)
    keys = cached_keys.astype(jnp.float32).reshape(CACHE, KVH, HD)
    values = cached_values.astype(jnp.float32).reshape(CACHE, KVH, HD)
    fresh_k = fresh_keys.astype(jnp.float32).reshape(STEPS, KVH, HD)
    fresh_v = fresh_values.astype(jnp.float32).reshape(STEPS, KVH, HD)
    old = jnp.einsum('tgjd,pgd->tgjp', q_all, keys) * scale
    new = jnp.einsum('tgjd,sgd->tgjs', q_all, fresh_k) * scale
    valid = (jnp.arange(CACHE, dtype=jnp.int32) < length)[None, None, None, :]
    causal = (jnp.arange(STEPS)[:, None] >= jnp.arange(STEPS)[None, :])[:, None, None, :]
    old = jnp.where(valid, old, NEG)
    new = jnp.where(causal, new, NEG)
    top = jnp.maximum(lax.optimization_barrier(jnp.max(old, axis=-1)), lax.optimization_barrier(jnp.max(new, axis=-1)))
    e_old = jnp.where(valid, jnp.exp(old - top[..., None]), 0.0)
    e_new = jnp.where(causal, jnp.exp(new - top[..., None]), 0.0)
    den = lax.optimization_barrier(jnp.sum(e_old, axis=-1)) + lax.optimization_barrier(jnp.sum(e_new, axis=-1))
    w_old = e_old.astype(jnp.bfloat16).astype(jnp.float32)
    w_new = e_new.astype(jnp.bfloat16).astype(jnp.float32)
    num = jnp.einsum('tgjp,pgd->tgjd', w_old, values) + jnp.einsum('tgjs,sgd->tgjd', w_new, fresh_v)
    return (num / den[..., None]).reshape(STEPS, QH * HD).astype(jnp.bfloat16)

def reference(decode_token_index, token_embedding_table, input_norm_scale, projection_weight, input_factor, output_factor, cache, cache_length_rows, queries):
    embedded = token_embedding_table[decode_token_index]
    wide = embedded.astype(jnp.float32)
    mean_sq = lax.optimization_barrier(jnp.mean(wide * wide, axis=-1, keepdims=True))
    normed = (wide * input_norm_scale.astype(jnp.float32) * lax.rsqrt(mean_sq + EPS)).astype(jnp.bfloat16)
    lowrank_update = jnp.einsum('amh,azm->ahz', input_factor.astype(jnp.float32), output_factor.astype(jnp.float32))
    merged = (projection_weight.astype(jnp.float32) + lowrank_update).astype(jnp.bfloat16)
    projected = jnp.einsum('atd,pdk->patk', normed.astype(jnp.float32), merged.astype(jnp.float32))
    positions = cache_length_rows[:, None] + jnp.arange(STEPS, dtype=jnp.int32)[None, :]
    new_kv = jnp.stack([rotate(projected[0], positions), projected[1]]).astype(jnp.bfloat16)
    attended = lax.map(attend_row, (queries, cache[0], cache[1], new_kv[0], new_kv[1], cache_length_rows))
    return (attended, new_kv)
```

```python
import functools
import math

import jax
import jax.numpy as jnp
from jax import lax
from jax.experimental import pallas as pl
from jax.experimental.pallas import tpu as pltpu
from jax.sharding import PartitionSpec as P

X, ZH, Y, C = 4, 2, 4, 2
T = 8
GROUP = ZH * Y * C
KVH = 4
QH = 32
HD = 128
ROPE_THETA = 1000000.0
NEG = -1e30
EPS = 1e-06
SHRINK = 2.0**-20
LANES = 128
MESH = pl.DeviceIdType.MESH
F32 = jnp.float32
BF16 = jnp.bfloat16


def iota(shape, dim):
    return lax.broadcasted_iota(jnp.int32, shape, dim)


def nt(a, b):
    return lax.dot_general(a, b, (((1,), (1,)), ((), ())), preferred_element_type=F32)


def tn(a, b):
    return lax.dot_general(a, b, (((0,), (0,)), ((), ())), preferred_element_type=F32)


def loop(lo, hi, fn):
    def step(i, carry):
        fn(i)
        return carry

    lax.fori_loop(lo, hi, step, 0)


def kernel(
    ids_ref, len_ref, gain_ref, a_ref, b_ref, table_hbm, w_hbm, cache_hbm, q_hbm,
    att_ref, kv_ref,
    table, weight, cache, q_in, load_sem,
    ids_one, ids_all, fac_one, fac_all, qs, qbd,
    core_out, core_in, plane_out, plane_in, merged,
    part_out, part_in, stat_out, stat_in, old_all, old_stat,
    kv_out, kv_in, sq_out, sq_in, kv_all,
    id1_s, id1_r, id2_s, id2_r, fa1_s, fa1_r, fa2_s, fa2_r,
    core_s, core_r, plane_s, plane_r, part_s, part_r, stat_s, stat_r,
    old_s, old_r, olst_s, olst_r, kv_s, kv_r, sq_s, sq_r, new_s, new_r,
):
    r = lax.axis_index("replica")
    t = lax.axis_index("tp")
    x = r // GROUP
    m = r % GROUP
    zh = m // (Y * C)
    y = (m // C) % Y
    c = m % C
    rows, steps = ids_ref.shape
    toks = rows * steps
    voc, feat = table.shape
    c_loc = cache.shape[2]
    features = feat * T
    my_row = t // 2
    pair = t % 2

    def rep(x_, zh_, y_, c_):
        return ((x_ * ZH + zh_) * Y + y_) * C + c_

    def remote(src, dst, send, recv, where):
        return pltpu.make_async_remote_copy(
            src_ref=src, dst_ref=dst, send_sem=send, recv_sem=recv,
            device_id=where, device_id_type=MESH,
        )

    loads = [
        pltpu.make_async_copy(q_hbm, q_in, load_sem.at[0]),
        pltpu.make_async_copy(cache_hbm, cache, load_sem.at[1]),
        pltpu.make_async_copy(table_hbm, table, load_sem.at[2]),
        pltpu.make_async_copy(w_hbm, weight, load_sem.at[3]),
    ]
    for load in loads:
        load.start()

    barrier = pltpu.get_barrier_semaphore()

    def hello(where):
        pl.semaphore_signal(barrier, inc=1, device_id=where, device_id_type=MESH)

    loop(1, GROUP, lambda d: hello((x * GROUP + (m + d) % GROUP, t)))
    loop(Y, X * Y, lambda d: hello((rep((x + d // Y) % X, zh, (y + d % Y) % Y, c), t)))
    loop(ZH, ZH * T, lambda d: hello((rep(x, (zh + d % ZH) % ZH, y, c), (t + d // ZH) % T)))

    lane = iota((1, LANES), 1)
    row = jnp.zeros((1, LANES), jnp.int32)
    base = (y * ZH + zh) * toks
    for k in range(toks):
        row = jnp.where(lane == base + k, ids_ref[k // steps, k % steps], row)
    ids_one[m] = row
    chunks = feat // LANES
    pieces = []
    for ref in (a_ref, b_ref):
        for p in range(2):
            for i in range(chunks):
                pieces.append(ref[p : p + 1, i * LANES : (i + 1) * LANES].astype(F32))
    fac_one[m] = jnp.concatenate(pieces, axis=0).astype(BF16)

    pl.semaphore_wait(barrier, (GROUP - 1) + (X - 1) * Y + (T - 1) * ZH)

    def id1(d):
        other = (m + d) % GROUP
        return remote(ids_one.at[m], ids_one.at[m], id1_s.at[d], id1_r.at[m], (x * GROUP + other, t))

    def id1_in(d):
        other = (m + d) % GROUP
        return remote(ids_one.at[m], ids_one.at[other], id1_s.at[d], id1_r.at[other], (x * GROUP + other, t))

    def fa1(d):
        other = (m + d) % GROUP
        return remote(fac_one.at[m], fac_one.at[m], fa1_s.at[d], fa1_r.at[m], (x * GROUP + other, t))

    def fa1_in(d):
        other = (m + d) % GROUP
        return remote(fac_one.at[m], fac_one.at[other], fa1_s.at[d], fa1_r.at[other], (x * GROUP + other, t))

    loop(1, GROUP, lambda d: id1(d).start())
    loop(1, GROUP, lambda d: fa1(d).start())

    loads[0].wait()
    qbd[...] = jnp.zeros_like(qbd)
    for a in range(rows):
        q32 = q_in[a].astype(F32)
        tall = jnp.concatenate([q32[:, h * HD : (h + 1) * HD] for h in range(QH)], axis=0).astype(BF16)
        qs[a] = tall
        span = tall.shape[0] // KVH
        for g in range(KVH):
            qbd[a, g * span : (g + 1) * span, g * HD : (g + 1) * HD] = tall[g * span : (g + 1) * span, :]
    loads[1].wait()
    scale = 1.0 / math.sqrt(HD)

    def attend(a):
        s = nt(cache[0, a], qbd[a]) * scale
        valid = t * c_loc + iota(s.shape, 0) < len_ref[a]
        s = jnp.where(valid, s, NEG)
        top = jnp.max(s, axis=0, keepdims=True)
        e = jnp.where(valid, jnp.exp(s - top), 0.0)
        den = jnp.sum(e, axis=0, keepdims=True)
        num = tn(e.astype(BF16), cache[1, a])
        span = num.shape[0] // KVH
        half = 2 * span
        for g in range(KVH):
            part_out[2 * a + g // 2, (g % 2) * span : (g % 2 + 1) * span, :] = num[
                g * span : (g + 1) * span, g * HD : (g + 1) * HD
            ].astype(BF16)
        stat_out[a] = jnp.concatenate([top, den], axis=0)

    def part(d):
        to = (t + d) % T
        return remote(part_out.at[to], part_in.at[t], part_s.at[d], part_r.at[t], (r, to))

    def part_wait(d):
        to = (t + d) % T
        return remote(part_out.at[to], part_in.at[to], part_s.at[d], part_r.at[to], (r, to))

    def stat(d):
        to = (t + d) % T
        return remote(stat_out.at[to // 2], stat_in.at[t], stat_s.at[d], stat_r.at[t], (r, to))

    def stat_wait(d):
        to = (t + d) % T
        return remote(stat_out.at[to // 2], stat_in.at[to], stat_s.at[d], stat_r.at[to], (r, to))

    loop(0, rows // 2, attend)

    loop(1, GROUP, lambda d: id1_in(d).wait_recv())
    gathered = []
    for c_ in range(C):
        total = ids_one[c_]
        for i in range(1, ZH * Y):
            total = total + ids_one[i * C + c_]
        gathered.append(total)
    ids_all[x] = jnp.concatenate(gathered, axis=0)

    def id2(d):
        return remote(ids_all.at[x], ids_all.at[x], id2_s.at[d], id2_r.at[x], (rep((x + d) % X, zh, y, c), t))

    def id2_in(d):
        other = (x + d) % X
        return remote(ids_all.at[x], ids_all.at[other], id2_s.at[d], id2_r.at[other], (rep(other, zh, y, c), t))

    loop(1, X, lambda d: id2(d).start())

    loop(1, GROUP, lambda d: fa1_in(d).wait_recv())
    size = GROUP * GROUP
    flat = fac_one[...].reshape(GROUP * 16, LANES)
    o, i = iota((16 * GROUP, 16 * GROUP), 0), iota((16 * GROUP, 16 * GROUP), 1)
    perm = ((o // GROUP == i % 16) & (o % GROUP == i // 16)).astype(F32).astype(BF16)
    fac_all[x] = jnp.dot(perm, flat, preferred_element_type=F32).astype(BF16).reshape(16, GROUP, LANES)

    def fa2(d):
        return remote(fac_all.at[x], fac_all.at[x], fa2_s.at[d], fa2_r.at[x], (rep((x + d) % X, zh, y, c), t))

    def fa2_in(d):
        other = (x + d) % X
        return remote(fac_all.at[x], fac_all.at[other], fa2_s.at[d], fa2_r.at[other], (rep(other, zh, y, c), t))

    loop(1, X, lambda d: fa2(d).start())

    loop(rows // 2, rows, attend)
    loop(1, T, lambda d: stat(d).start())
    loop(1, T, lambda d: part(d).start())

    loop(1, X, lambda d: id2_in(d).wait_recv())
    loads[2].wait()
    start = r * voc

    def lookup(x_, c_):
        wide = jnp.broadcast_to(ids_all[x_, pl.ds(c_, 1), :], (LANES, LANES))
        ids = jnp.transpose(wide)[:, 0:1] - start
        onehot = (ids == iota((LANES, voc), 1)).astype(F32).astype(BF16)
        return jnp.dot(onehot, table[...], preferred_element_type=F32)

    share = ZH * toks

    def core(k):
        return remote(core_out.at[k], core_in.at[k], core_s.at[k], core_r.at[k], (rep(x, zh, y, 1 - c), t))

    def first(k):
        core_out[k] = lookup((x + 1 + k) % X, 1 - c).astype(BF16)
        core(k).start()

    loop(0, X, first)

    def plane(d):
        dx, dy = d // Y, d % Y
        x_, y_ = (x + dx) % X, (y + dy) % Y
        return remote(
            plane_out.at[dx, y_], plane_in.at[x * Y + y], plane_s.at[d], plane_r.at[x * Y + y],
            (rep(x_, zh, y_, c), t),
        )

    def plane_wait(d):
        x_, y_ = (x + d // Y) % X, (y + d % Y) % Y
        slot = x_ * Y + y_
        return remote(
            plane_out.at[d // Y, y_], plane_in.at[slot], plane_s.at[d], plane_r.at[slot],
            (rep(x_, zh, y_, c), t),
        )

    def second(k):
        dx = (1 + k) % X
        found = lookup((x + dx) % X, c)
        core(k).wait_recv()
        plane_out[dx] = (found + core_in[k].astype(F32)).astype(BF16).reshape(Y, share, feat)

    def second_far(k):
        second(k)
        loop(0, Y, lambda dy: plane((1 + k) * Y + dy).start())

    loop(0, X - 1, second_far)
    second(X - 1)
    loop(1, Y, lambda dy: plane(dy).start())

    loop(1, X, lambda d: fa2_in(d).wait_recv())
    loads[3].wait()
    for p in range(2):
        full = []
        for side in range(2):
            full.append(
                jnp.concatenate(
                    [
                        fac_all[:, (side * 2 + p) * chunks + i].reshape(X * GROUP, LANES)
                        for i in range(chunks)
                    ],
                    axis=1,
                )
            )
        update = tn(full[0], full[1])
        merged[p] = (weight[p].astype(F32) + update).astype(BF16)

    loop(1, T, lambda d: stat_wait(d).wait_recv())
    stat_in[t] = stat_out[my_row]
    tops = jnp.concatenate([stat_in[i][0:1] for i in range(T)], axis=0)
    dens = jnp.concatenate([stat_in[i][1:2] for i in range(T)], axis=0)
    top = jnp.max(tops, axis=0, keepdims=True)
    w = jnp.exp(tops - top)
    den = jnp.sum(dens * w, axis=0, keepdims=True)
    old_stat[t] = jnp.concatenate([top, den], axis=0)
    w = jnp.transpose(jnp.concatenate([w / den, jnp.zeros((LANES - T, LANES), F32)], axis=0))
    w = jnp.where(pair == 0, w[: LANES // 2], w[LANES // 2 :])
    loop(1, T, lambda d: part_wait(d).wait_recv())
    part_in[t] = part_out[t]
    mix = part_in[0].astype(F32) * w[:, 0:1]
    for i in range(1, T):
        mix = mix + part_in[i].astype(F32) * w[:, i : i + 1]
    old_all[t] = mix.astype(BF16)

    def old(d):
        to = (t + d) % T
        return remote(old_all.at[t], old_all.at[t], old_s.at[d], old_r.at[t], (r, to))

    def old_wait(d):
        to = (t + d) % T
        return remote(old_all.at[t], old_all.at[to], old_s.at[d], old_r.at[to], (r, to))

    def olst(d):
        to = (t + d) % T
        return remote(old_stat.at[t], old_stat.at[t], olst_s.at[d], olst_r.at[t], (r, to))

    def olst_wait(d):
        to = (t + d) % T
        return remote(old_stat.at[t], old_stat.at[to], olst_s.at[d], olst_r.at[to], (r, to))

    loop(1, T, lambda d: olst(d).start())
    loop(1, T, lambda d: old(d).start())

    half = HD // 2
    keyed = 2 * steps
    position = (len_ref[my_row] + iota((keyed, HD), 0) % steps).astype(F32)
    column = iota((keyed, HD), 1)
    freq = jnp.exp((column % half).astype(F32) * (-2.0 * math.log(ROPE_THETA) / HD))
    angle = position * freq
    cosine = jnp.cos(angle)
    sine = jnp.where(column < half, -jnp.sin(angle), jnp.sin(angle))

    loop(1, X * Y, lambda d: plane_wait(d).wait_recv())
    plane_in[x * Y + y] = plane_out[0, y]
    embedded = plane_in[0].astype(F32)
    for i in range(1, X * Y):
        embedded = embedded + plane_in[i].astype(F32)
    squares = jnp.sum(embedded * embedded, axis=1, keepdims=True)
    squares = jnp.where(iota((share, LANES), 0) == iota((share, LANES), 1), squares, 0.0)
    sq_out[...] = jnp.sum(squares, axis=0, keepdims=True)
    ready = (embedded * (gain_ref[...].astype(F32) * SHRINK)).astype(BF16)
    proj = [jnp.dot(ready, merged[p], preferred_element_type=F32) for p in range(2)]
    for zh_ in range(ZH):
        for t_ in range(T):
            at = zh_ * toks + (t_ // 2) * steps
            cols = (t_ % 2) * 2 * HD
            kv_out[zh_, t_] = jnp.concatenate(
                [
                    proj[p][at : at + steps, cols + i * HD : cols + (i + 1) * HD]
                    for p in range(2)
                    for i in range(2)
                ],
                axis=0,
            ).astype(BF16)

    def ring(d):
        return (zh + d // T) % ZH, (t + d % T) % T

    def kv(d):
        zh_, t_ = ring(d)
        me = zh * T + t
        return remote(kv_out.at[zh_, t_], kv_in.at[me], kv_s.at[d], kv_r.at[me], (rep(x, zh_, y, c), t_))

    def kv_wait(d):
        zh_, t_ = ring(d)
        slot = zh_ * T + t_
        return remote(kv_out.at[zh_, t_], kv_in.at[slot], kv_s.at[d], kv_r.at[slot], (rep(x, zh_, y, c), t_))

    def sq(d):
        zh_, t_ = ring(d)
        me = zh * T + t
        return remote(sq_out, sq_in.at[me], sq_s.at[d], sq_r.at[me], (rep(x, zh_, y, c), t_))

    def sq_wait(d):
        zh_, t_ = ring(d)
        slot = zh_ * T + t_
        return remote(sq_out, sq_in.at[slot], sq_s.at[d], sq_r.at[slot], (rep(x, zh_, y, c), t_))

    loop(1, ZH * T, lambda d: sq(d).start())
    loop(1, ZH * T, lambda d: kv(d).start())
    kv_in[zh * T + t] = kv_out[zh, t]
    sq_in[zh * T + t] = sq_out[...]

    loop(1, ZH * T, lambda d: sq_wait(d).wait_recv())
    sq_sum = sq_in[0]
    for i in range(1, ZH * T):
        sq_sum = sq_sum + sq_in[i]
    inverse = lax.rsqrt(sq_sum / features + EPS) * (1.0 / SHRINK)
    keep = iota((4 * steps, LANES), 1) == zh * toks + my_row * steps + iota((4 * steps, LANES), 0) % steps
    factor = jnp.sum(jnp.where(keep, inverse, 0.0), axis=1, keepdims=True)
    loop(1, ZH * T, lambda d: kv_wait(d).wait_recv())
    fresh = kv_in[0].astype(F32)
    for i in range(1, ZH * T):
        fresh = fresh + kv_in[i].astype(F32)
    fresh = fresh * factor
    keys = fresh[:keyed]
    keys = keys * cosine + pltpu.roll(keys, half, 1) * sine
    kv_all[t] = jnp.concatenate([keys, fresh[keyed:]], axis=0).astype(BF16)

    def new(d):
        to = (t + d) % T
        return remote(kv_all.at[t], kv_all.at[t], new_s.at[d], new_r.at[t], (r, to))

    def new_wait(d):
        to = (t + d) % T
        return remote(kv_all.at[t], kv_all.at[to], new_s.at[d], new_r.at[to], (r, to))

    loop(1, T, lambda d: new(d).start())

    loop(1, T, lambda d: olst_wait(d).wait_recv())
    loop(1, T, lambda d: old_wait(d).wait_recv())
    loop(1, T, lambda d: new_wait(d).wait_recv())
    at_lane = iota((keyed, LANES), 1)
    at_row = iota((keyed, LANES), 0)
    span = LANES // KVH
    causal = (at_row // steps == (at_lane // span) % 2) & (at_row % steps <= at_lane % steps)
    low = lane < LANES // 2
    shares, news = [], []
    for a in range(rows):
        s = jnp.where(
            at_lane < LANES // 2, nt(kv_all[2 * a], qs[a])[:keyed], nt(kv_all[2 * a + 1], qs[a])[:keyed]
        ) * scale
        s = jnp.where(causal, s, NEG)
        stats = jnp.where(low, old_stat[2 * a], old_stat[2 * a + 1])
        old_top, old_den = stats[0:1], stats[1:2]
        top = jnp.maximum(old_top, jnp.max(s, axis=0, keepdims=True))
        e = jnp.where(causal, jnp.exp(s - top), 0.0)
        old_den = old_den * jnp.exp(old_top - top)
        den = old_den + jnp.sum(e, axis=0, keepdims=True)
        shares.append(old_den / den)
        news.append(e / den)
    cols = jnp.transpose(jnp.concatenate(shares + [jnp.zeros((LANES - rows, LANES), F32)], axis=0))
    for a in range(rows):
        e = jnp.concatenate([jnp.zeros_like(news[a]), news[a]], axis=0).astype(BF16)
        lower = tn(e, kv_all[2 * a])[: LANES // 2]
        upper = tn(e, kv_all[2 * a + 1])[LANES // 2 :]
        add = jnp.concatenate([lower, upper], axis=0)
        oldies = jnp.concatenate([old_all[2 * a], old_all[2 * a + 1]], axis=0).astype(F32)
        out = oldies * cols[:, a : a + 1] + add
        for h in range(QH):
            att_ref[a, :, h * HD : (h + 1) * HD] = out[h * steps : (h + 1) * steps].astype(BF16)
        for g in range(KVH):
            got = kv_all[2 * a + g // 2].astype(F32)
            for p in range(2):
                at = (p * 2 + g % 2) * steps
                kv_ref[p, a, :, g * HD : (g + 1) * HD] = got[at : at + steps].astype(BF16)

    loop(1, GROUP, lambda d: id1(d).wait_send())
    loop(1, GROUP, lambda d: fa1(d).wait_send())
    loop(1, X, lambda d: id2(d).wait_send())
    loop(1, X, lambda d: fa2(d).wait_send())
    loop(0, X, lambda d: core(d).wait_send())
    loop(1, X * Y, lambda d: plane(d).wait_send())
    loop(1, T, lambda d: stat(d).wait_send())
    loop(1, T, lambda d: part(d).wait_send())
    loop(1, T, lambda d: olst(d).wait_send())
    loop(1, T, lambda d: old(d).wait_send())
    loop(1, ZH * T, lambda d: sq(d).wait_send())
    loop(1, ZH * T, lambda d: kv(d).wait_send())
    loop(1, T, lambda d: new(d).wait_send())


def shards(ids, table, gain, weight, in_factor, out_factor, cache, lengths, queries):
    rows, steps = ids.shape
    voc, feat = table.shape
    vmem = pl.BlockSpec(memory_space=pltpu.VMEM)
    smem = pl.BlockSpec(memory_space=pltpu.SMEM)
    hbm = pl.BlockSpec(memory_space=pl.ANY)
    share = ZH * rows * steps
    dma = pltpu.SemaphoreType.DMA
    half = LANES // 2
    scratch = [
        pltpu.VMEM(table.shape, BF16),
        pltpu.VMEM(weight.shape, BF16),
        pltpu.VMEM(cache.shape, BF16),
        pltpu.VMEM(queries.shape, BF16),
        dma((4,)),
        pltpu.VMEM((GROUP, 1, LANES), jnp.int32),
        pltpu.VMEM((X, C, LANES), jnp.int32),
        pltpu.VMEM((GROUP, 16, LANES), BF16),
        pltpu.VMEM((X, 16, GROUP, LANES), BF16),
        pltpu.VMEM((rows, LANES, HD), BF16),
        pltpu.VMEM((rows, LANES, KVH * HD), BF16),
        pltpu.VMEM((X, LANES, feat), BF16),
        pltpu.VMEM((X, LANES, feat), BF16),
        pltpu.VMEM((X, Y, share, feat), BF16),
        pltpu.VMEM((X * Y, share, feat), BF16),
        pltpu.VMEM(weight.shape, BF16),
        pltpu.VMEM((T, half, HD), BF16),
        pltpu.VMEM((T, half, HD), BF16),
        pltpu.VMEM((rows, 2, LANES), F32),
        pltpu.VMEM((T, 2, LANES), F32),
        pltpu.VMEM((T, half, HD), BF16),
        pltpu.VMEM((T, 2, LANES), F32),
        pltpu.VMEM((ZH, T, 4 * steps, HD), BF16),
        pltpu.VMEM((ZH * T, 4 * steps, HD), BF16),
        pltpu.VMEM((1, LANES), F32),
        pltpu.VMEM((ZH * T, 1, LANES), F32),
        pltpu.VMEM((T, 4 * steps, HD), BF16),
    ]
    for count in (GROUP, GROUP, X, X, GROUP, GROUP, X, X, X, X, X * Y, X * Y, T, T, T, T):
        scratch.append(dma((count,)))
    for count in (T, T, T, T, ZH * T, ZH * T, ZH * T, ZH * T, T, T):
        scratch.append(dma((count,)))
    return pl.pallas_call(
        kernel,
        out_shape=(
            jax.ShapeDtypeStruct((rows, steps, QH * HD), BF16),
            jax.ShapeDtypeStruct((2, rows, steps, KVH * HD), BF16),
        ),
        in_specs=[smem, smem, vmem, vmem, vmem, hbm, hbm, hbm, hbm],
        out_specs=(vmem, vmem),
        scratch_shapes=scratch,
        compiler_params=pltpu.CompilerParams(
            collective_id=0, has_side_effects=True, vmem_limit_bytes=48 * 1024 * 1024
        ),
        cost_estimate=pl.CostEstimate(flops=2_000_000_000, bytes_accessed=5_000_000, transcendentals=200_000),
    )(
        ids,
        lengths,
        gain.reshape(1, feat),
        in_factor.reshape(2, feat),
        out_factor.reshape(2, feat),
        table,
        weight,
        cache,
        queries,
    )


def solution(mesh):
    placed = (
        P("replica", None),
        P("replica", "tp"),
        P("tp"),
        P(None, "tp", None),
        P(None, "replica", "tp"),
        P(None, None, "replica"),
        P(None, "replica", "tp", None),
        P("replica"),
        P("replica", None, None),
    )
    return jax.shard_map(
        shards,
        mesh=mesh,
        in_specs=placed,
        out_specs=(P("replica", None, None), P(None, "replica", None, None)),
        check_vma=False,
    )
```

```python
import functools
import math

import jax
import jax.numpy as jnp
from jax import lax
from jax.experimental import pallas as pl
from jax.experimental.pallas import tpu as pltpu
from jax.sharding import PartitionSpec as P

X, ZH, Y, C = 4, 2, 4, 2
T = 8
GROUP = ZH * Y * C
KVH = 4
QH = 32
HD = 128
ROPE_THETA = 1000000.0
NEG = -1e30
EPS = 1e-06
SHRINK = 2.0**-20
LANES = 128
MESH = pl.DeviceIdType.MESH
F32 = jnp.float32
BF16 = jnp.bfloat16


def iota(shape, dim):
    return lax.broadcasted_iota(jnp.int32, shape, dim)


def nt(a, b):
    return lax.dot_general(a, b, (((1,), (1,)), ((), ())), preferred_element_type=F32)


def tn(a, b):
    return lax.dot_general(a, b, (((0,), (0,)), ((), ())), preferred_element_type=F32)


def loop(lo, hi, fn):
    def step(i, carry):
        fn(i)
        return carry

    lax.fori_loop(lo, hi, step, 0)


def kernel(
    ids_hbm, len_hbm, gain_hbm, a_hbm, b_hbm, table_hbm, w_hbm, cache_hbm, q_hbm,
    att_ref, kv_ref,
    ids_ref, len_ref, gain_ref, a_ref, b_ref, table, weight, cache, q_in, load_sem,
    ids_one, ids_all, fac_one, fac_all, qs, qbd,
    core_out, core_in, plane_out, plane_in, merged,
    part_out, part_in, stat_out, stat_in, old_all, old_stat,
    kv_out, kv_in, sq_out, sq_in, kv_all,
    id1_s, id1_r, id2_s, id2_r, fa1_s, fa1_r, fa2_s, fa2_r,
    core_s, core_r, plane_s, plane_r, part_s, part_r, stat_s, stat_r,
    old_s, old_r, olst_s, olst_r, kv_s, kv_r, sq_s, sq_r, new_s, new_r,
):
    r = lax.axis_index("replica")
    t = lax.axis_index("tp")
    x = r // GROUP
    m = r % GROUP
    zh = m // (Y * C)
    y = (m // C) % Y
    c = m % C
    rows, steps = ids_ref.shape
    toks = rows * steps
    voc, feat = table.shape
    c_loc = cache.shape[2]
    features = feat * T
    my_row = t // 2
    pair = t % 2

    def rep(x_, zh_, y_, c_):
        return ((x_ * ZH + zh_) * Y + y_) * C + c_

    def remote(src, dst, send, recv, where):
        return pltpu.make_async_remote_copy(
            src_ref=src, dst_ref=dst, send_sem=send, recv_sem=recv,
            device_id=where, device_id_type=MESH,
        )

    loads = [
        pltpu.make_async_copy(q_hbm, q_in, load_sem.at[0]),
        pltpu.make_async_copy(cache_hbm, cache, load_sem.at[1]),
        pltpu.make_async_copy(table_hbm, table, load_sem.at[2]),
        pltpu.make_async_copy(w_hbm, weight, load_sem.at[3]),
        pltpu.make_async_copy(len_hbm, len_ref, load_sem.at[4]),
        pltpu.make_async_copy(gain_hbm, gain_ref, load_sem.at[5]),
    ]
    urgent = [
        pltpu.make_async_copy(ids_hbm, ids_ref, load_sem.at[6]),
        pltpu.make_async_copy(a_hbm, a_ref, load_sem.at[7]),
        pltpu.make_async_copy(b_hbm, b_ref, load_sem.at[8]),
    ]
    for load in urgent:
        load.start()
    for load in loads:
        load.start()

    barrier = pltpu.get_barrier_semaphore()

    def hello(where):
        pl.semaphore_signal(barrier, inc=1, device_id=where, device_id_type=MESH)

    loop(1, GROUP, lambda d: hello((x * GROUP + (m + d) % GROUP, t)))
    loop(Y, X * Y, lambda d: hello((rep((x + d // Y) % X, zh, (y + d % Y) % Y, c), t)))
    loop(ZH, ZH * T, lambda d: hello((rep(x, (zh + d % ZH) % ZH, y, c), (t + d // ZH) % T)))

    for load in urgent:
        load.wait()
    lane = iota((1, LANES), 1)
    row = jnp.zeros((1, LANES), jnp.int32)
    base = (y * ZH + zh) * toks
    for k in range(toks):
        row = jnp.where(lane == base + k, ids_ref[k // steps, k % steps], row)
    ids_one[m] = row
    chunks = feat // LANES
    pieces = []
    for ref in (a_ref, b_ref):
        for p in range(2):
            for i in range(chunks):
                pieces.append(ref[p : p + 1, i * LANES : (i + 1) * LANES].astype(F32))
    fac_one[m] = jnp.concatenate(pieces, axis=0).astype(BF16)

    pl.semaphore_wait(barrier, (GROUP - 1) + (X - 1) * Y + (T - 1) * ZH)

    def id1(d):
        other = (m + d) % GROUP
        return remote(ids_one.at[m], ids_one.at[m], id1_s.at[d], id1_r.at[m], (x * GROUP + other, t))

    def id1_in(d):
        other = (m + d) % GROUP
        return remote(ids_one.at[m], ids_one.at[other], id1_s.at[d], id1_r.at[other], (x * GROUP + other, t))

    def fa1(d):
        other = (m + d) % GROUP
        return remote(fac_one.at[m], fac_one.at[m], fa1_s.at[d], fa1_r.at[m], (x * GROUP + other, t))

    def fa1_in(d):
        other = (m + d) % GROUP
        return remote(fac_one.at[m], fac_one.at[other], fa1_s.at[d], fa1_r.at[other], (x * GROUP + other, t))

    loop(1, GROUP, lambda d: id1(d).start())
    loop(1, GROUP, lambda d: fa1(d).start())

    loads[0].wait()
    qbd[...] = jnp.zeros_like(qbd)
    for a in range(rows):
        q32 = q_in[a].astype(F32)
        tall = jnp.concatenate([q32[:, h * HD : (h + 1) * HD] for h in range(QH)], axis=0).astype(BF16)
        qs[a] = tall
        span = tall.shape[0] // KVH
        for g in range(KVH):
            qbd[a, g * span : (g + 1) * span, g * HD : (g + 1) * HD] = tall[g * span : (g + 1) * span, :]
    loads[1].wait()
    loads[4].wait()
    scale = 1.0 / math.sqrt(HD)

    def attend(a):
        s = nt(cache[0, a], qbd[a]) * scale
        valid = t * c_loc + iota(s.shape, 0) < len_ref[a]
        s = jnp.where(valid, s, NEG)
        top = jnp.max(s, axis=0, keepdims=True)
        e = jnp.where(valid, jnp.exp(s - top), 0.0)
        den = jnp.sum(e, axis=0, keepdims=True)
        num = tn(e.astype(BF16), cache[1, a])
        span = num.shape[0] // KVH
        half = 2 * span
        for g in range(KVH):
            part_out[2 * a + g // 2, (g % 2) * span : (g % 2 + 1) * span, :] = num[
                g * span : (g + 1) * span, g * HD : (g + 1) * HD
            ].astype(BF16)
        stat_out[a] = jnp.concatenate([top, den], axis=0)

    def part(d):
        to = (t + d) % T
        return remote(part_out.at[to], part_in.at[t], part_s.at[d], part_r.at[t], (r, to))

    def part_wait(d):
        to = (t + d) % T
        return remote(part_out.at[to], part_in.at[to], part_s.at[d], part_r.at[to], (r, to))

    def stat(d):
        to = (t + d) % T
        return remote(stat_out.at[to // 2], stat_in.at[t], stat_s.at[d], stat_r.at[t], (r, to))

    def stat_wait(d):
        to = (t + d) % T
        return remote(stat_out.at[to // 2], stat_in.at[to], stat_s.at[d], stat_r.at[to], (r, to))

    loop(0, rows // 2, attend)

    loop(1, GROUP, lambda d: id1_in(d).wait_recv())
    gathered = []
    for c_ in range(C):
        total = ids_one[c_]
        for i in range(1, ZH * Y):
            total = total + ids_one[i * C + c_]
        gathered.append(total)
    ids_all[x] = jnp.concatenate(gathered, axis=0)

    def id2(d):
        return remote(ids_all.at[x], ids_all.at[x], id2_s.at[d], id2_r.at[x], (rep((x + d) % X, zh, y, c), t))

    def id2_in(d):
        other = (x + d) % X
        return remote(ids_all.at[x], ids_all.at[other], id2_s.at[d], id2_r.at[other], (rep(other, zh, y, c), t))

    loop(1, X, lambda d: id2(d).start())

    loop(1, GROUP, lambda d: fa1_in(d).wait_recv())
    size = GROUP * GROUP
    flat = fac_one[...].reshape(GROUP * 16, LANES)
    o, i = iota((16 * GROUP, 16 * GROUP), 0), iota((16 * GROUP, 16 * GROUP), 1)
    perm = ((o // GROUP == i % 16) & (o % GROUP == i // 16)).astype(F32).astype(BF16)
    fac_all[x] = jnp.dot(perm, flat, preferred_element_type=F32).astype(BF16).reshape(16, GROUP, LANES)

    def fa2(d):
        return remote(fac_all.at[x], fac_all.at[x], fa2_s.at[d], fa2_r.at[x], (rep((x + d) % X, zh, y, c), t))

    def fa2_in(d):
        other = (x + d) % X
        return remote(fac_all.at[x], fac_all.at[other], fa2_s.at[d], fa2_r.at[other], (rep(other, zh, y, c), t))

    loop(1, X, lambda d: fa2(d).start())

    loop(rows // 2, rows, attend)
    loop(1, T, lambda d: stat(d).start())
    loop(1, T, lambda d: part(d).start())

    loop(1, X, lambda d: id2_in(d).wait_recv())
    loads[2].wait()
    start = r * voc

    def lookup(x_, c_):
        wide = jnp.broadcast_to(ids_all[x_, pl.ds(c_, 1), :], (LANES, LANES))
        ids = jnp.transpose(wide)[:, 0:1] - start
        onehot = (ids == iota((LANES, voc), 1)).astype(F32).astype(BF16)
        return jnp.dot(onehot, table[...], preferred_element_type=F32)

    share = ZH * toks

    def core(k):
        return remote(core_out.at[k], core_in.at[k], core_s.at[k], core_r.at[k], (rep(x, zh, y, 1 - c), t))

    def first(k):
        core_out[k] = lookup((x + 1 + k) % X, 1 - c).astype(BF16)
        core(k).start()

    loop(0, X, first)

    def plane(d):
        dx, dy = d // Y, d % Y
        x_, y_ = (x + dx) % X, (y + dy) % Y
        return remote(
            plane_out.at[dx, y_], plane_in.at[x * Y + y], plane_s.at[d], plane_r.at[x * Y + y],
            (rep(x_, zh, y_, c), t),
        )

    def plane_wait(d):
        x_, y_ = (x + d // Y) % X, (y + d % Y) % Y
        slot = x_ * Y + y_
        return remote(
            plane_out.at[d // Y, y_], plane_in.at[slot], plane_s.at[d], plane_r.at[slot],
            (rep(x_, zh, y_, c), t),
        )

    def second(k):
        dx = (1 + k) % X
        found = lookup((x + dx) % X, c)
        core(k).wait_recv()
        plane_out[dx] = (found + core_in[k].astype(F32)).astype(BF16).reshape(Y, share, feat)

    def second_far(k):
        second(k)
        loop(0, Y, lambda dy: plane((1 + k) * Y + dy).start())

    loop(0, X - 1, second_far)
    second(X - 1)
    loop(1, Y, lambda dy: plane(dy).start())

    loop(1, X, lambda d: fa2_in(d).wait_recv())
    loads[3].wait()
    loads[5].wait()
    for p in range(2):
        full = []
        for side in range(2):
            full.append(
                jnp.concatenate(
                    [
                        fac_all[:, (side * 2 + p) * chunks + i].reshape(X * GROUP, LANES)
                        for i in range(chunks)
                    ],
                    axis=1,
                )
            )
        update = tn(full[0], full[1])
        merged[p] = (weight[p].astype(F32) + update).astype(BF16)

    loop(1, T, lambda d: stat_wait(d).wait_recv())
    stat_in[t] = stat_out[my_row]
    tops = jnp.concatenate([stat_in[i][0:1] for i in range(T)], axis=0)
    dens = jnp.concatenate([stat_in[i][1:2] for i in range(T)], axis=0)
    top = jnp.max(tops, axis=0, keepdims=True)
    w = jnp.exp(tops - top)
    den = jnp.sum(dens * w, axis=0, keepdims=True)
    old_stat[t] = jnp.concatenate([top, den], axis=0)
    w = jnp.transpose(jnp.concatenate([w / den, jnp.zeros((LANES - T, LANES), F32)], axis=0))
    w = jnp.where(pair == 0, w[: LANES // 2], w[LANES // 2 :])
    loop(1, T, lambda d: part_wait(d).wait_recv())
    part_in[t] = part_out[t]
    mix = part_in[0].astype(F32) * w[:, 0:1]
    for i in range(1, T):
        mix = mix + part_in[i].astype(F32) * w[:, i : i + 1]
    old_all[t] = mix.astype(BF16)

    def old(d):
        to = (t + d) % T
        return remote(old_all.at[t], old_all.at[t], old_s.at[d], old_r.at[t], (r, to))

    def old_wait(d):
        to = (t + d) % T
        return remote(old_all.at[t], old_all.at[to], old_s.at[d], old_r.at[to], (r, to))

    def olst(d):
        to = (t + d) % T
        return remote(old_stat.at[t], old_stat.at[t], olst_s.at[d], olst_r.at[t], (r, to))

    def olst_wait(d):
        to = (t + d) % T
        return remote(old_stat.at[t], old_stat.at[to], olst_s.at[d], olst_r.at[to], (r, to))

    loop(1, T, lambda d: olst(d).start())
    loop(1, T, lambda d: old(d).start())

    half = HD // 2
    keyed = 2 * steps
    position = (len_ref[my_row] + iota((keyed, HD), 0) % steps).astype(F32)
    column = iota((keyed, HD), 1)
    freq = jnp.exp((column % half).astype(F32) * (-2.0 * math.log(ROPE_THETA) / HD))
    angle = position * freq
    cosine = jnp.cos(angle)
    sine = jnp.where(column < half, -jnp.sin(angle), jnp.sin(angle))

    loop(1, X * Y, lambda d: plane_wait(d).wait_recv())
    plane_in[x * Y + y] = plane_out[0, y]
    embedded = plane_in[0].astype(F32)
    for i in range(1, X * Y):
        embedded = embedded + plane_in[i].astype(F32)
    gain = gain_ref[...].astype(F32)
    gain = jnp.concatenate([gain[i : i + 1] for i in range(chunks)], axis=1)
    squares = jnp.sum(embedded * embedded, axis=1, keepdims=True)
    squares = jnp.where(iota((share, LANES), 0) == iota((share, LANES), 1), squares, 0.0)
    sq_out[...] = jnp.sum(squares, axis=0, keepdims=True)
    ready = (embedded * (gain * SHRINK)).astype(BF16)
    proj = [jnp.dot(ready, merged[p], preferred_element_type=F32) for p in range(2)]
    for zh_ in range(ZH):
        for t_ in range(T):
            at = zh_ * toks + (t_ // 2) * steps
            cols = (t_ % 2) * 2 * HD
            kv_out[zh_, t_] = jnp.concatenate(
                [
                    proj[p][at : at + steps, cols + i * HD : cols + (i + 1) * HD]
                    for p in range(2)
                    for i in range(2)
                ],
                axis=0,
            ).astype(BF16)

    def ring(d):
        return (zh + d // T) % ZH, (t + d % T) % T

    def kv(d):
        zh_, t_ = ring(d)
        me = zh * T + t
        return remote(kv_out.at[zh_, t_], kv_in.at[me], kv_s.at[d], kv_r.at[me], (rep(x, zh_, y, c), t_))

    def kv_wait(d):
        zh_, t_ = ring(d)
        slot = zh_ * T + t_
        return remote(kv_out.at[zh_, t_], kv_in.at[slot], kv_s.at[d], kv_r.at[slot], (rep(x, zh_, y, c), t_))

    def sq(d):
        zh_, t_ = ring(d)
        me = zh * T + t
        return remote(sq_out, sq_in.at[me], sq_s.at[d], sq_r.at[me], (rep(x, zh_, y, c), t_))

    def sq_wait(d):
        zh_, t_ = ring(d)
        slot = zh_ * T + t_
        return remote(sq_out, sq_in.at[slot], sq_s.at[d], sq_r.at[slot], (rep(x, zh_, y, c), t_))

    loop(1, ZH * T, lambda d: sq(d).start())
    loop(1, ZH * T, lambda d: kv(d).start())
    kv_in[zh * T + t] = kv_out[zh, t]
    sq_in[zh * T + t] = sq_out[...]

    loop(1, ZH * T, lambda d: sq_wait(d).wait_recv())
    sq_sum = sq_in[0]
    for i in range(1, ZH * T):
        sq_sum = sq_sum + sq_in[i]
    inverse = lax.rsqrt(sq_sum / features + EPS) * (1.0 / SHRINK)
    keep = iota((4 * steps, LANES), 1) == zh * toks + my_row * steps + iota((4 * steps, LANES), 0) % steps
    factor = jnp.sum(jnp.where(keep, inverse, 0.0), axis=1, keepdims=True)
    loop(1, ZH * T, lambda d: kv_wait(d).wait_recv())
    fresh = kv_in[0].astype(F32)
    for i in range(1, ZH * T):
        fresh = fresh + kv_in[i].astype(F32)
    fresh = fresh * factor
    keys = fresh[:keyed]
    keys = keys * cosine + pltpu.roll(keys, half, 1) * sine
    kv_all[t] = jnp.concatenate([keys, fresh[keyed:]], axis=0).astype(BF16)

    def new(d):
        to = (t + d) % T
        return remote(kv_all.at[t], kv_all.at[t], new_s.at[d], new_r.at[t], (r, to))

    def new_wait(d):
        to = (t + d) % T
        return remote(kv_all.at[t], kv_all.at[to], new_s.at[d], new_r.at[to], (r, to))

    loop(1, T, lambda d: new(d).start())

    loop(1, T, lambda d: olst_wait(d).wait_recv())
    loop(1, T, lambda d: old_wait(d).wait_recv())
    loop(1, T, lambda d: new_wait(d).wait_recv())
    at_lane = iota((keyed, LANES), 1)
    at_row = iota((keyed, LANES), 0)
    span = LANES // KVH
    causal = (at_row // steps == (at_lane // span) % 2) & (at_row % steps <= at_lane % steps)
    low = lane < LANES // 2
    shares, news = [], []
    for a in range(rows):
        s = jnp.where(
            at_lane < LANES // 2, nt(kv_all[2 * a], qs[a])[:keyed], nt(kv_all[2 * a + 1], qs[a])[:keyed]
        ) * scale
        s = jnp.where(causal, s, NEG)
        stats = jnp.where(low, old_stat[2 * a], old_stat[2 * a + 1])
        old_top, old_den = stats[0:1], stats[1:2]
        top = jnp.maximum(old_top, jnp.max(s, axis=0, keepdims=True))
        e = jnp.where(causal, jnp.exp(s - top), 0.0)
        old_den = old_den * jnp.exp(old_top - top)
        den = old_den + jnp.sum(e, axis=0, keepdims=True)
        shares.append(old_den / den)
        news.append(e / den)
    cols = jnp.transpose(jnp.concatenate(shares + [jnp.zeros((LANES - rows, LANES), F32)], axis=0))
    for a in range(rows):
        e = jnp.concatenate([jnp.zeros_like(news[a]), news[a]], axis=0).astype(BF16)
        lower = tn(e, kv_all[2 * a])[: LANES // 2]
        upper = tn(e, kv_all[2 * a + 1])[LANES // 2 :]
        add = jnp.concatenate([lower, upper], axis=0)
        oldies = jnp.concatenate([old_all[2 * a], old_all[2 * a + 1]], axis=0).astype(F32)
        out = oldies * cols[:, a : a + 1] + add
        for h in range(QH):
            att_ref[a, :, h * HD : (h + 1) * HD] = out[h * steps : (h + 1) * steps].astype(BF16)
        for g in range(KVH):
            got = kv_all[2 * a + g // 2].astype(F32)
            for p in range(2):
                at = (p * 2 + g % 2) * steps
                kv_ref[p, a, :, g * HD : (g + 1) * HD] = got[at : at + steps].astype(BF16)

    loop(1, GROUP, lambda d: id1(d).wait_send())
    loop(1, GROUP, lambda d: fa1(d).wait_send())
    loop(1, X, lambda d: id2(d).wait_send())
    loop(1, X, lambda d: fa2(d).wait_send())
    loop(0, X, lambda d: core(d).wait_send())
    loop(1, X * Y, lambda d: plane(d).wait_send())
    loop(1, T, lambda d: stat(d).wait_send())
    loop(1, T, lambda d: part(d).wait_send())
    loop(1, T, lambda d: olst(d).wait_send())
    loop(1, T, lambda d: old(d).wait_send())
    loop(1, ZH * T, lambda d: sq(d).wait_send())
    loop(1, ZH * T, lambda d: kv(d).wait_send())
    loop(1, T, lambda d: new(d).wait_send())


def shards(ids, table, gain, weight, in_factor, out_factor, cache, lengths, queries):
    rows, steps = ids.shape
    voc, feat = table.shape
    vmem = pl.BlockSpec(memory_space=pltpu.VMEM)
    hbm = pl.BlockSpec(memory_space=pltpu.HBM)
    share = ZH * rows * steps
    dma = pltpu.SemaphoreType.DMA
    half = LANES // 2
    scratch = [
        pltpu.SMEM(ids.shape, jnp.int32),
        pltpu.SMEM(lengths.shape, jnp.int32),
        pltpu.VMEM((feat // LANES, LANES), BF16),
        pltpu.VMEM((2, feat), BF16),
        pltpu.VMEM((2, feat), BF16),
        pltpu.VMEM(table.shape, BF16),
        pltpu.VMEM(weight.shape, BF16),
        pltpu.VMEM(cache.shape, BF16),
        pltpu.VMEM(queries.shape, BF16),
        dma((9,)),
        pltpu.VMEM((GROUP, 1, LANES), jnp.int32),
        pltpu.VMEM((X, C, LANES), jnp.int32),
        pltpu.VMEM((GROUP, 16, LANES), BF16),
        pltpu.VMEM((X, 16, GROUP, LANES), BF16),
        pltpu.VMEM((rows, LANES, HD), BF16),
        pltpu.VMEM((rows, LANES, KVH * HD), BF16),
        pltpu.VMEM((X, LANES, feat), BF16),
        pltpu.VMEM((X, LANES, feat), BF16),
        pltpu.VMEM((X, Y, share, feat), BF16),
        pltpu.VMEM((X * Y, share, feat), BF16),
        pltpu.VMEM(weight.shape, BF16),
        pltpu.VMEM((T, half, HD), BF16),
        pltpu.VMEM((T, half, HD), BF16),
        pltpu.VMEM((rows, 2, LANES), F32),
        pltpu.VMEM((T, 2, LANES), F32),
        pltpu.VMEM((T, half, HD), BF16),
        pltpu.VMEM((T, 2, LANES), F32),
        pltpu.VMEM((ZH, T, 4 * steps, HD), BF16),
        pltpu.VMEM((ZH * T, 4 * steps, HD), BF16),
        pltpu.VMEM((1, LANES), F32),
        pltpu.VMEM((ZH * T, 1, LANES), F32),
        pltpu.VMEM((T, 4 * steps, HD), BF16),
    ]
    for count in (GROUP, GROUP, X, X, GROUP, GROUP, X, X, X, X, X * Y, X * Y, T, T, T, T):
        scratch.append(dma((count,)))
    for count in (T, T, T, T, ZH * T, ZH * T, ZH * T, ZH * T, T, T):
        scratch.append(dma((count,)))
    return pl.pallas_call(
        kernel,
        out_shape=(
            jax.ShapeDtypeStruct((rows, steps, QH * HD), BF16),
            jax.ShapeDtypeStruct((2, rows, steps, KVH * HD), BF16),
        ),
        in_specs=[hbm] * 9,
        out_specs=(vmem, vmem),
        scratch_shapes=scratch,
        compiler_params=pltpu.CompilerParams(
            collective_id=0, has_side_effects=True, vmem_limit_bytes=60 * 1024 * 1024
        ),
        cost_estimate=pl.CostEstimate(flops=2_000_000_000, bytes_accessed=5_000_000, transcendentals=200_000),
    )(
        ids,
        lengths,
        gain.reshape(feat // LANES, LANES),
        in_factor.reshape(2, feat),
        out_factor.reshape(2, feat),
        table,
        weight,
        cache,
        queries,
    )


def solution(mesh):
    placed = (
        P("replica", None),
        P("replica", "tp"),
        P("tp"),
        P(None, "tp", None),
        P(None, "replica", "tp"),
        P(None, None, "replica"),
        P(None, "replica", "tp", None),
        P("replica"),
        P("replica", None, None),
    )
    return jax.shard_map(
        shards,
        mesh=mesh,
        in_specs=placed,
        out_specs=(P("replica", None, None), P(None, "replica", None, None)),
        check_vma=False,
    )
```

```python
import functools
import math

import jax
import jax.numpy as jnp
from jax import lax
from jax.experimental import pallas as pl
from jax.experimental.pallas import tpu as pltpu
from jax.sharding import PartitionSpec as P

X, ZH, Y, C = 4, 2, 4, 2
T = 8
GROUP = ZH * Y * C
KVH = 4
QH = 32
HD = 128
ROPE_THETA = 1000000.0
NEG = -1e30
EPS = 1e-06
SHRINK = 2.0**-20
LANES = 128
MESH = pl.DeviceIdType.MESH
F32 = jnp.float32
BF16 = jnp.bfloat16


def iota(shape, dim):
    return lax.broadcasted_iota(jnp.int32, shape, dim)


def nt(a, b):
    return lax.dot_general(a, b, (((1,), (1,)), ((), ())), preferred_element_type=F32)


def tn(a, b):
    return lax.dot_general(a, b, (((0,), (0,)), ((), ())), preferred_element_type=F32)


def loop(lo, hi, fn):
    def step(i, carry):
        fn(i)
        return carry

    lax.fori_loop(lo, hi, step, 0)


def kernel(
    ids_hbm, len_hbm, gain_hbm, a_hbm, b_hbm, table_hbm, w_hbm, cache_hbm, q_hbm,
    att_ref, kv_ref,
    ids_ref, len_ref, gain_ref, a_ref, b_ref, table, weight, cache, q_in, load_sem,
    ids_one, ids_all, fac_one, fac_all, qs, qbd,
    core_out, core_in, plane_out, plane_in, merged,
    part_out, part_in, stat_out, stat_in, old_all, old_stat,
    kv_out, kv_in, sq_out, sq_in, kv_all,
    id1_s, id1_r, id2_s, id2_r, fa1_s, fa1_r, fa2_s, fa2_r,
    core_s, core_r, plane_s, plane_r, part_s, part_r, stat_s, stat_r,
    old_s, old_r, olst_s, olst_r, kv_s, kv_r, sq_s, sq_r, new_s, new_r,
):
    r = lax.axis_index("replica")
    t = lax.axis_index("tp")
    x = r // GROUP
    m = r % GROUP
    zh = m // (Y * C)
    y = (m // C) % Y
    c = m % C
    rows, steps = ids_ref.shape
    toks = rows * steps
    voc, feat = table.shape
    c_loc = cache.shape[2]
    features = feat * T
    my_row = t // 2
    pair = t % 2

    def rep(x_, zh_, y_, c_):
        return ((x_ * ZH + zh_) * Y + y_) * C + c_

    def remote(src, dst, send, recv, where):
        return pltpu.make_async_remote_copy(
            src_ref=src, dst_ref=dst, send_sem=send, recv_sem=recv,
            device_id=where, device_id_type=MESH,
        )

    loads = [
        pltpu.make_async_copy(q_hbm, q_in, load_sem.at[0]),
        pltpu.make_async_copy(cache_hbm, cache, load_sem.at[1]),
        pltpu.make_async_copy(table_hbm, table, load_sem.at[2]),
        pltpu.make_async_copy(w_hbm, weight, load_sem.at[3]),
        pltpu.make_async_copy(len_hbm, len_ref, load_sem.at[4]),
        pltpu.make_async_copy(gain_hbm, gain_ref, load_sem.at[5]),
    ]
    urgent = [
        pltpu.make_async_copy(ids_hbm, ids_ref, load_sem.at[6]),
        pltpu.make_async_copy(a_hbm, a_ref, load_sem.at[7]),
        pltpu.make_async_copy(b_hbm, b_ref, load_sem.at[8]),
    ]
    for load in urgent:
        load.start()
    for load in loads:
        load.start()

    barrier = pltpu.get_barrier_semaphore()

    def hello(where):
        pl.semaphore_signal(barrier, inc=1, device_id=where, device_id_type=MESH)

    loop(1, GROUP, lambda d: hello((x * GROUP + (m + d) % GROUP, t)))
    loop(Y, X * Y, lambda d: hello((rep((x + d // Y) % X, zh, (y + d % Y) % Y, c), t)))
    loop(ZH, ZH * T, lambda d: hello((rep(x, (zh + d % ZH) % ZH, y, c), (t + d // ZH) % T)))

    for load in urgent:
        load.wait()
    lane = iota((1, LANES), 1)
    row = jnp.zeros((1, LANES), jnp.int32)
    base = (y * ZH + zh) * toks
    for k in range(toks):
        row = jnp.where(lane == base + k, ids_ref[k // steps, k % steps], row)
    ids_one[m] = row
    chunks = feat // LANES
    pieces = []
    for ref in (a_ref, b_ref):
        for p in range(2):
            for i in range(chunks):
                pieces.append(ref[p : p + 1, i * LANES : (i + 1) * LANES].astype(F32))
    fac_one[m] = jnp.concatenate(pieces, axis=0).astype(BF16)

    pl.semaphore_wait(barrier, (GROUP - 1) + (X - 1) * Y + (T - 1) * ZH)

    def id1(d):
        other = (m + d) % GROUP
        return remote(ids_one.at[m], ids_one.at[m], id1_s.at[d], id1_r.at[m], (x * GROUP + other, t))

    def id1_in(d):
        other = (m + d) % GROUP
        return remote(ids_one.at[m], ids_one.at[other], id1_s.at[d], id1_r.at[other], (x * GROUP + other, t))

    def fa1(d):
        other = (m + d) % GROUP
        return remote(fac_one.at[m], fac_one.at[m], fa1_s.at[d], fa1_r.at[m], (x * GROUP + other, t))

    def fa1_in(d):
        other = (m + d) % GROUP
        return remote(fac_one.at[m], fac_one.at[other], fa1_s.at[d], fa1_r.at[other], (x * GROUP + other, t))

    loop(1, GROUP, lambda d: id1(d).start())
    loop(1, GROUP, lambda d: fa1(d).start())

    loads[0].wait()
    qbd[...] = jnp.zeros_like(qbd)
    for a in range(rows):
        q32 = q_in[a].astype(F32)
        tall = jnp.concatenate([q32[:, h * HD : (h + 1) * HD] for h in range(QH)], axis=0).astype(BF16)
        qs[a] = tall
        span = tall.shape[0] // KVH
        for g in range(KVH):
            qbd[a, g * span : (g + 1) * span, g * HD : (g + 1) * HD] = tall[g * span : (g + 1) * span, :]
    loads[1].wait()
    loads[4].wait()
    scale = 1.0 / math.sqrt(HD)

    def attend(a):
        s = nt(cache[0, a], qbd[a]) * scale
        valid = t * c_loc + iota(s.shape, 0) < len_ref[a]
        s = jnp.where(valid, s, NEG)
        top = jnp.max(s, axis=0, keepdims=True)
        e = jnp.where(valid, jnp.exp(s - top), 0.0)
        den = jnp.sum(e, axis=0, keepdims=True)
        num = tn(e.astype(BF16), cache[1, a])
        span = num.shape[0] // KVH
        half = 2 * span
        for g in range(KVH):
            part_out[2 * a + g // 2, (g % 2) * span : (g % 2 + 1) * span, :] = num[
                g * span : (g + 1) * span, g * HD : (g + 1) * HD
            ].astype(BF16)
        stat_out[a] = jnp.concatenate([top, den], axis=0)

    def part(d):
        to = (t + d) % T
        return remote(part_out.at[to], part_in.at[t], part_s.at[d], part_r.at[t], (r, to))

    def part_wait(d):
        to = (t + d) % T
        return remote(part_out.at[to], part_in.at[to], part_s.at[d], part_r.at[to], (r, to))

    def stat(d):
        to = (t + d) % T
        return remote(stat_out.at[to // 2], stat_in.at[t], stat_s.at[d], stat_r.at[t], (r, to))

    def stat_wait(d):
        to = (t + d) % T
        return remote(stat_out.at[to // 2], stat_in.at[to], stat_s.at[d], stat_r.at[to], (r, to))

    loop(0, rows // 2, attend)

    loop(1, GROUP, lambda d: id1_in(d).wait_recv())
    gathered = []
    for c_ in range(C):
        total = ids_one[c_]
        for i in range(1, ZH * Y):
            total = total + ids_one[i * C + c_]
        gathered.append(total)
    ids_all[x] = jnp.concatenate(gathered, axis=0)

    def id2(d):
        return remote(ids_all.at[x], ids_all.at[x], id2_s.at[d], id2_r.at[x], (rep((x + d) % X, zh, y, c), t))

    def id2_in(d):
        other = (x + d) % X
        return remote(ids_all.at[x], ids_all.at[other], id2_s.at[d], id2_r.at[other], (rep(other, zh, y, c), t))

    loop(1, X, lambda d: id2(d).start())

    loop(1, GROUP, lambda d: fa1_in(d).wait_recv())
    size = GROUP * GROUP
    flat = fac_one[...].reshape(GROUP * 16, LANES)
    o, i = iota((16 * GROUP, 16 * GROUP), 0), iota((16 * GROUP, 16 * GROUP), 1)
    perm = ((o // GROUP == i % 16) & (o % GROUP == i // 16)).astype(F32).astype(BF16)
    fac_all[x] = jnp.dot(perm, flat, preferred_element_type=F32).astype(BF16).reshape(16, GROUP, LANES)

    def fa2(d):
        return remote(fac_all.at[x], fac_all.at[x], fa2_s.at[d], fa2_r.at[x], (rep((x + d) % X, zh, y, c), t))

    def fa2_in(d):
        other = (x + d) % X
        return remote(fac_all.at[x], fac_all.at[other], fa2_s.at[d], fa2_r.at[other], (rep(other, zh, y, c), t))

    loop(1, X, lambda d: fa2(d).start())

    loop(rows // 2, rows, attend)
    loop(1, T, lambda d: stat(d).start())
    loop(1, T, lambda d: part(d).start())

    loop(1, X, lambda d: id2_in(d).wait_recv())
    loads[2].wait()
    start = r * voc

    def lookup(x_, c_):
        wide = jnp.broadcast_to(ids_all[x_, pl.ds(c_, 1), :], (LANES, LANES))
        ids = jnp.transpose(wide)[:, 0:1] - start
        onehot = (ids == iota((LANES, voc), 1)).astype(F32).astype(BF16)
        return jnp.dot(onehot, table[...], preferred_element_type=F32)

    share = ZH * toks

    def core(k):
        return remote(core_out.at[k], core_in.at[k], core_s.at[k], core_r.at[k], (rep(x, zh, y, 1 - c), t))

    def first(k):
        core_out[k] = lookup((x + 1 + k) % X, 1 - c).astype(BF16)
        core(k).start()

    loop(0, X, first)

    def plane(d):
        dx, dy = d // Y, d % Y
        x_, y_ = (x + dx) % X, (y + dy) % Y
        return remote(
            plane_out.at[dx, y_], plane_in.at[x * Y + y], plane_s.at[d], plane_r.at[x * Y + y],
            (rep(x_, zh, y_, c), t),
        )

    def plane_wait(d):
        x_, y_ = (x + d // Y) % X, (y + d % Y) % Y
        slot = x_ * Y + y_
        return remote(
            plane_out.at[d // Y, y_], plane_in.at[slot], plane_s.at[d], plane_r.at[slot],
            (rep(x_, zh, y_, c), t),
        )

    def second(k):
        dx = (1 + k) % X
        found = lookup((x + dx) % X, c)
        core(k).wait_recv()
        plane_out[dx] = (found + core_in[k].astype(F32)).astype(BF16).reshape(Y, share, feat)

    def second_far(k):
        second(k)
        loop(0, Y, lambda dy: plane((1 + k) * Y + dy).start())

    loop(0, X - 1, second_far)
    second(X - 1)
    loop(1, Y, lambda dy: plane(dy).start())

    loop(1, X, lambda d: fa2_in(d).wait_recv())
    loads[3].wait()
    loads[5].wait()
    for p in range(2):
        full = []
        for side in range(2):
            full.append(
                jnp.concatenate(
                    [
                        fac_all[:, (side * 2 + p) * chunks + i].reshape(X * GROUP, LANES)
                        for i in range(chunks)
                    ],
                    axis=1,
                )
            )
        update = tn(full[0], full[1])
        merged[p] = (weight[p].astype(F32) + update).astype(BF16)

    loop(1, T, lambda d: stat_wait(d).wait_recv())
    stat_in[t] = stat_out[my_row]
    tops = jnp.concatenate([stat_in[i][0:1] for i in range(T)], axis=0)
    dens = jnp.concatenate([stat_in[i][1:2] for i in range(T)], axis=0)
    top = jnp.max(tops, axis=0, keepdims=True)
    w = jnp.exp(tops - top)
    den = jnp.sum(dens * w, axis=0, keepdims=True)
    old_stat[t] = jnp.concatenate([top, den], axis=0)
    w = jnp.transpose(jnp.concatenate([w / den, jnp.zeros((LANES - T, LANES), F32)], axis=0))
    w = jnp.where(pair == 0, w[: LANES // 2], w[LANES // 2 :])
    loop(1, T, lambda d: part_wait(d).wait_recv())
    part_in[t] = part_out[t]
    mix = part_in[0].astype(F32) * w[:, 0:1]
    for i in range(1, T):
        mix = mix + part_in[i].astype(F32) * w[:, i : i + 1]
    old_all[t] = mix.astype(BF16)

    def old(d):
        to = (t + d) % T
        return remote(old_all.at[t], old_all.at[t], old_s.at[d], old_r.at[t], (r, to))

    def old_wait(d):
        to = (t + d) % T
        return remote(old_all.at[t], old_all.at[to], old_s.at[d], old_r.at[to], (r, to))

    def olst(d):
        to = (t + d) % T
        return remote(old_stat.at[t], old_stat.at[t], olst_s.at[d], olst_r.at[t], (r, to))

    def olst_wait(d):
        to = (t + d) % T
        return remote(old_stat.at[t], old_stat.at[to], olst_s.at[d], olst_r.at[to], (r, to))

    loop(1, T, lambda d: olst(d).start())
    loop(1, T, lambda d: old(d).start())

    half = HD // 2
    keyed = 2 * steps
    position = (len_ref[my_row] + iota((keyed, HD), 0) % steps).astype(F32)
    column = iota((keyed, HD), 1)
    freq = jnp.exp((column % half).astype(F32) * (-2.0 * math.log(ROPE_THETA) / HD))
    angle = position * freq
    cosine = jnp.cos(angle)
    sine = jnp.where(column < half, -jnp.sin(angle), jnp.sin(angle))

    loop(1, X * Y, lambda d: plane_wait(d).wait_recv())
    plane_in[x * Y + y] = plane_out[0, y]
    embedded = plane_in[0].astype(F32)
    for i in range(1, X * Y):
        embedded = embedded + plane_in[i].astype(F32)
    gain = gain_ref[...].astype(F32)
    gain = jnp.concatenate([gain[i : i + 1] for i in range(chunks)], axis=1)
    squares = jnp.sum(embedded * embedded, axis=1, keepdims=True)
    squares = jnp.where(iota((share, LANES), 0) == iota((share, LANES), 1), squares, 0.0)
    sq_out[...] = jnp.sum(squares, axis=0, keepdims=True)
    ready = (embedded * (gain * SHRINK)).astype(BF16)
    proj = [jnp.dot(ready, merged[p], preferred_element_type=F32) for p in range(2)]
    for zh_ in range(ZH):
        for t_ in range(T):
            at = zh_ * toks + (t_ // 2) * steps
            cols = (t_ % 2) * 2 * HD
            kv_out[zh_, t_] = jnp.concatenate(
                [
                    proj[p][at : at + steps, cols + i * HD : cols + (i + 1) * HD]
                    for p in range(2)
                    for i in range(2)
                ],
                axis=0,
            ).astype(BF16)

    def ring(d):
        return (zh + d // T) % ZH, (t + d % T) % T

    def kv(d):
        zh_, t_ = ring(d)
        me = zh * T + t
        return remote(kv_out.at[zh_, t_], kv_in.at[me], kv_s.at[d], kv_r.at[me], (rep(x, zh_, y, c), t_))

    def kv_wait(d):
        zh_, t_ = ring(d)
        slot = zh_ * T + t_
        return remote(kv_out.at[zh_, t_], kv_in.at[slot], kv_s.at[d], kv_r.at[slot], (rep(x, zh_, y, c), t_))

    def sq(d):
        zh_, t_ = ring(d)
        me = zh * T + t
        return remote(sq_out, sq_in.at[me], sq_s.at[d], sq_r.at[me], (rep(x, zh_, y, c), t_))

    def sq_wait(d):
        zh_, t_ = ring(d)
        slot = zh_ * T + t_
        return remote(sq_out, sq_in.at[slot], sq_s.at[d], sq_r.at[slot], (rep(x, zh_, y, c), t_))

    loop(1, ZH * T, lambda d: sq(d).start())
    loop(1, ZH * T, lambda d: kv(d).start())
    kv_in[zh * T + t] = kv_out[zh, t]
    sq_in[zh * T + t] = sq_out[...]

    loop(1, ZH * T, lambda d: sq_wait(d).wait_recv())
    sq_sum = sq_in[0]
    for i in range(1, ZH * T):
        sq_sum = sq_sum + sq_in[i]
    inverse = lax.rsqrt(sq_sum / features + EPS) * (1.0 / SHRINK)
    keep = iota((4 * steps, LANES), 1) == zh * toks + my_row * steps + iota((4 * steps, LANES), 0) % steps
    factor = jnp.sum(jnp.where(keep, inverse, 0.0), axis=1, keepdims=True)
    loop(1, ZH * T, lambda d: kv_wait(d).wait_recv())
    fresh = kv_in[0].astype(F32)
    for i in range(1, ZH * T):
        fresh = fresh + kv_in[i].astype(F32)
    fresh = fresh * factor
    keys = fresh[:keyed]
    keys = keys * cosine + pltpu.roll(keys, half, 1) * sine
    kv_all[t] = jnp.concatenate([keys, fresh[keyed:]], axis=0).astype(BF16)

    def new(d):
        to = (t + d) % T
        return remote(kv_all.at[t], kv_all.at[t], new_s.at[d], new_r.at[t], (r, to))

    def new_wait(d):
        to = (t + d) % T
        return remote(kv_all.at[t], kv_all.at[to], new_s.at[d], new_r.at[to], (r, to))

    loop(1, T, lambda d: new(d).start())

    loop(1, T, lambda d: olst_wait(d).wait_recv())
    loop(1, T, lambda d: old_wait(d).wait_recv())
    loop(1, T, lambda d: new_wait(d).wait_recv())
    at_lane = iota((keyed, LANES), 1)
    at_row = iota((keyed, LANES), 0)
    span = LANES // KVH
    causal = (at_row // steps == (at_lane // span) % 2) & (at_row % steps <= at_lane % steps)
    low = lane < LANES // 2
    shares, news = [], []
    for a in range(rows):
        s = jnp.where(
            at_lane < LANES // 2, nt(kv_all[2 * a], qs[a])[:keyed], nt(kv_all[2 * a + 1], qs[a])[:keyed]
        ) * scale
        s = jnp.where(causal, s, NEG)
        stats = jnp.where(low, old_stat[2 * a], old_stat[2 * a + 1])
        old_top, old_den = stats[0:1], stats[1:2]
        top = jnp.maximum(old_top, jnp.max(s, axis=0, keepdims=True))
        e = jnp.where(causal, jnp.exp(s - top), 0.0)
        old_den = old_den * jnp.exp(old_top - top)
        den = old_den + jnp.sum(e, axis=0, keepdims=True)
        shares.append(old_den / den)
        news.append(e / den)
    cols = jnp.transpose(jnp.concatenate(shares + [jnp.zeros((LANES - rows, LANES), F32)], axis=0))
    for a in range(rows):
        e = jnp.concatenate([jnp.zeros_like(news[a]), news[a]], axis=0).astype(BF16)
        lower = tn(e, kv_all[2 * a])[: LANES // 2]
        upper = tn(e, kv_all[2 * a + 1])[LANES // 2 :]
        add = jnp.concatenate([lower, upper], axis=0)
        oldies = jnp.concatenate([old_all[2 * a], old_all[2 * a + 1]], axis=0).astype(F32)
        out = oldies * cols[:, a : a + 1] + add
        for h in range(QH):
            att_ref[a, :, h * HD : (h + 1) * HD] = out[h * steps : (h + 1) * steps].astype(BF16)
        for g in range(KVH):
            got = kv_all[2 * a + g // 2].astype(F32)
            for p in range(2):
                at = (p * 2 + g % 2) * steps
                kv_ref[p, a, :, g * HD : (g + 1) * HD] = got[at : at + steps].astype(BF16)

    loop(1, GROUP, lambda d: id1(d).wait_send())
    loop(1, GROUP, lambda d: fa1(d).wait_send())
    loop(1, X, lambda d: id2(d).wait_send())
    loop(1, X, lambda d: fa2(d).wait_send())
    loop(0, X, lambda d: core(d).wait_send())
    loop(1, X * Y, lambda d: plane(d).wait_send())
    loop(1, T, lambda d: stat(d).wait_send())
    loop(1, T, lambda d: part(d).wait_send())
    loop(1, T, lambda d: olst(d).wait_send())
    loop(1, T, lambda d: old(d).wait_send())
    loop(1, ZH * T, lambda d: sq(d).wait_send())
    loop(1, ZH * T, lambda d: kv(d).wait_send())
    loop(1, T, lambda d: new(d).wait_send())


def deliver(att_in, kv_in, att_out, kv_out):
    att_out[...] = att_in[...]
    kv_out[...] = kv_in[...]


def shards(ids, table, gain, weight, in_factor, out_factor, cache, lengths, queries):
    rows, steps = ids.shape
    voc, feat = table.shape
    vmem = pl.BlockSpec(memory_space=pltpu.VMEM)
    hbm = pl.BlockSpec(memory_space=pltpu.HBM)
    share = ZH * rows * steps
    dma = pltpu.SemaphoreType.DMA
    half = LANES // 2
    scratch = [
        pltpu.SMEM(ids.shape, jnp.int32),
        pltpu.SMEM(lengths.shape, jnp.int32),
        pltpu.VMEM((feat // LANES, LANES), BF16),
        pltpu.VMEM((2, feat), BF16),
        pltpu.VMEM((2, feat), BF16),
        pltpu.VMEM(table.shape, BF16),
        pltpu.VMEM(weight.shape, BF16),
        pltpu.VMEM(cache.shape, BF16),
        pltpu.VMEM(queries.shape, BF16),
        dma((9,)),
        pltpu.VMEM((GROUP, 1, LANES), jnp.int32),
        pltpu.VMEM((X, C, LANES), jnp.int32),
        pltpu.VMEM((GROUP, 16, LANES), BF16),
        pltpu.VMEM((X, 16, GROUP, LANES), BF16),
        pltpu.VMEM((rows, LANES, HD), BF16),
        pltpu.VMEM((rows, LANES, KVH * HD), BF16),
        pltpu.VMEM((X, LANES, feat), BF16),
        pltpu.VMEM((X, LANES, feat), BF16),
        pltpu.VMEM((X, Y, share, feat), BF16),
        pltpu.VMEM((X * Y, share, feat), BF16),
        pltpu.VMEM(weight.shape, BF16),
        pltpu.VMEM((T, half, HD), BF16),
        pltpu.VMEM((T, half, HD), BF16),
        pltpu.VMEM((rows, 2, LANES), F32),
        pltpu.VMEM((T, 2, LANES), F32),
        pltpu.VMEM((T, half, HD), BF16),
        pltpu.VMEM((T, 2, LANES), F32),
        pltpu.VMEM((ZH, T, 4 * steps, HD), BF16),
        pltpu.VMEM((ZH * T, 4 * steps, HD), BF16),
        pltpu.VMEM((1, LANES), F32),
        pltpu.VMEM((ZH * T, 1, LANES), F32),
        pltpu.VMEM((T, 4 * steps, HD), BF16),
    ]
    for count in (GROUP, GROUP, X, X, GROUP, GROUP, X, X, X, X, X * Y, X * Y, T, T, T, T):
        scratch.append(dma((count,)))
    for count in (T, T, T, T, ZH * T, ZH * T, ZH * T, ZH * T, T, T):
        scratch.append(dma((count,)))
    made = pl.pallas_call(
        kernel,
        out_shape=(
            jax.ShapeDtypeStruct((rows, steps, QH * HD), BF16),
            jax.ShapeDtypeStruct((2, rows, steps, KVH * HD), BF16),
        ),
        in_specs=[hbm] * 9,
        out_specs=(vmem, vmem),
        scratch_shapes=scratch,
        compiler_params=pltpu.CompilerParams(
            collective_id=0, has_side_effects=True, vmem_limit_bytes=60 * 1024 * 1024
        ),
        cost_estimate=pl.CostEstimate(flops=2_000_000_000, bytes_accessed=5_000_000, transcendentals=200_000),
    )(
        ids,
        lengths,
        gain.reshape(feat // LANES, LANES),
        in_factor.reshape(2, feat),
        out_factor.reshape(2, feat),
        table,
        weight,
        cache,
        queries,
    )
    return pl.pallas_call(
        deliver,
        out_shape=tuple(jax.ShapeDtypeStruct(one.shape, one.dtype) for one in made),
        in_specs=[vmem, vmem],
        out_specs=(vmem, vmem),
        compiler_params=pltpu.CompilerParams(vmem_limit_bytes=60 * 1024 * 1024),
    )(*made)


def solution(mesh):
    placed = (
        P("replica", None),
        P("replica", "tp"),
        P("tp"),
        P(None, "tp", None),
        P(None, "replica", "tp"),
        P(None, None, "replica"),
        P(None, "replica", "tp", None),
        P("replica"),
        P("replica", None, None),
    )
    return jax.shard_map(
        shards,
        mesh=mesh,
        in_specs=placed,
        out_specs=(P("replica", None, None), P(None, "replica", None, None)),
        check_vma=False,
    )
```
